32 devices in a mesh: dp: 16 (over z, y, core), mp: 2 (over x).
Axes of the slice: x: 2, y: 2, z: 4, core: 2. Of those that a mesh axis runs over, the one named last changes fastest.
Arguments:
- hidden_states: bfloat16 [8192, 2560], P('dp'), may hold values from -16 to 16
- head_weight: bfloat16 [2560, 1024], P(None, 'mp'), may hold values from -1 to 1
- agent_bias: float32 [8, 1024], P(None, 'mp'), may hold values from -6 to 6
- agent_ids: int32 [8192], P('dp'), may hold values from 0 to 7
- actions: int32 [8192], P('dp'), may hold values from 0 to 1023
- rewards: float32 [8192], P('dp'), may hold values from -18 to 18
- values: float32 [8192], P('dp'), may hold values from -6 to 6
- episode_start: int32 [8192], P('dp'), may hold values 0 or 1
- prior_ratio: float32 [8192], P('dp'), may hold values from 0.5 to 2
- sample_rows: int32 [32768], P('dp'), may hold values from 0 to 8191, as said below
Outputs:
- natural_step: float32 [2560, 1024], P(None, 'mp')
The draws below stay inside these ranges and needn't reach their ends.
Inputs may be any that keep to these rules, and one draw needn't show every extreme that they name: `sample_rows`: each aligned block of 2048 entries names rows of the matching block of 512 rows of hidden_states; a row may be named more than once.
All inputs are finite; a program needn't handle non-finite values. No bound on the sum of `episode_start` on one device may be relied on, other than what follows from the above.
Results may differ from the reference program's by a relative error of at most 0.003.
Values may be sent and summed in bfloat16 or wider, within the bound.
No kernel may reach another device: no remote copies, remote signals or barrier semaphores. Data moves between devices by JAX's collectives and lax.ppermute only.
A program may use at most 128 MiB of HBM per device.

```python
import math
import jax
import jax.numpy as jnp
import numpy as np
from jax import lax

D = 2560
A = 1024
AGENTS = 8
SEQ_LEN = 64
ITERS = 2
TOK_DEV = 512
SAMP_DEV = 2048
TOKENS = 8192
SAMPLES = 32768


def shared_base(key):
    key_states, key_weights = jax.random.split(jax.random.fold_in(key, 11))
    states = jnp.clip(jax.random.normal(key_states, (TOKENS, D), jnp.float32), -6.0, 6.0)
    weights = jnp.clip(jax.random.normal(key_weights, (D, A), jnp.float32), -6.0, 6.0) / math.sqrt(D)
    return (states, weights)


def draw_hidden_states(key, part):
    states, weights = shared_base(key)
    return states.astype(jnp.bfloat16)


def draw_head_weight(key, part):
    states, weights = shared_base(key)
    return weights.astype(jnp.bfloat16)


def draw_rewards(key, part):
    positions = jnp.arange(TOKENS, dtype=jnp.int32)
    blocks = TOKENS // TOK_DEV
    scale = 1.0 + 2.0 * (positions // TOK_DEV).astype(jnp.float32) / max(blocks - 1, 1)
    reward_key = jax.random.fold_in(key, 23)
    base = jnp.clip(jax.random.normal(reward_key, (TOKENS,), jnp.float32), -6.0, 6.0)
    return base * scale


def draw_sample_rows(key, part):
    total = SAMP_DEV * (TOKENS // TOK_DEV)
    positions = jnp.arange(total, dtype=jnp.int32)
    owner = positions // SAMP_DEV
    offset = positions % SAMP_DEV
    within = jax.random.randint(jax.random.fold_in(key, 31), (total,), 0, TOK_DEV, dtype=jnp.int32)
    within = jnp.where(offset == 0, jnp.int32(0), within)
    within = jnp.where(offset == SAMP_DEV - 1, jnp.int32(TOK_DEV - 1), within)
    return owner * TOK_DEV + within


def plant(entries, rng, least, top_value):
    place = [jax.random.randint(jax.random.fold_in(rng, axis), (), 0, length) for axis, length in enumerate(entries.shape)]
    longest = entries.shape.index(max(entries.shape))
    beside = place[:longest] + [(place[longest] + 1) % entries.shape[longest]] + place[longest + 1:]
    return entries.at[tuple(place)].set(least).at[tuple(beside)].set(top_value)


def steps_of(key, shape, cuts, low, top_value):
    factor_of, own = 1.0, jax.random.fold_in(key, 6)
    for position, shards_of in cuts:
        heights = jnp.exp(jax.random.uniform(jax.random.fold_in(own, position), (shards_of,), jnp.float32, low / len(cuts), top_value / len(cuts)))
        factor_of = factor_of * jnp.repeat(heights, shape[position] // shards_of).reshape([-1 if axis == position else 1 for axis in range(len(shape))])
    return factor_of


def cumulative_ranks(count, slope):
    portions = [(1 << 20) // math.isqrt(rank ** slope) + 1 for rank in range(1, count + 1)]
    spread = 1 + sum(portions) // (1 << 30)
    return np.cumsum(np.array([max(1, weight // spread) for weight in portions]))


def ranked_ids(own_key, shape, number_of, slope):
    grid = cumulative_ranks(number_of, slope)
    ticket = jax.random.randint(jax.random.fold_in(own_key, 1), shape, 0, int(grid[number_of - 1]))
    rank = jnp.searchsorted(jnp.asarray(grid, jnp.int32), ticket, side="right")
    return jax.random.permutation(jax.random.fold_in(own_key, 2), number_of)[rank].astype(jnp.int32)


def gaussian(key, extent, deviation, bound, shards=(), kind=jnp.bfloat16):
    level = steps_of(key, extent, shards, -0.22, 0.18) if shards else 1.0
    values = jax.random.normal(key, extent, jnp.float32) * deviation * level
    return jnp.minimum(jnp.maximum(values, -bound), bound).astype(kind)


def setup_inputs(seed: int = 0) -> dict:
    key_list = jax.random.split(jax.random.key(seed), 11)
    hidden_states = draw_hidden_states(jax.random.fold_in(key_list[10], 71), 0)
    head_weight = draw_head_weight(jax.random.fold_in(key_list[10], 71), 0)
    agent_bias = gaussian(key_list[2], (AGENTS, A), 1.0, 6.0, ((1, 2),), jnp.float32)
    agent_ids = plant(jax.random.randint(key_list[3], (TOKENS,), 0, AGENTS), jax.random.fold_in(key_list[3], 1), 0, AGENTS - 1).astype(jnp.int32)
    actions = plant(ranked_ids(key_list[4], (TOKENS,), A, 2), jax.random.fold_in(key_list[4], 3), 0, A - 1).astype(jnp.int32)
    rewards = draw_rewards(jax.random.fold_in(key_list[10], 71), 0)
    values = gaussian(key_list[6], (TOKENS,), 1.0, 6.0, ((0, 16),), jnp.float32)
    episode_start = plant((jax.random.randint(key_list[7], (TOKENS,), 0, 16) < 1).astype(jnp.int32), jax.random.fold_in(key_list[7], 1), 0, 1)
    prior_ratio = jnp.clip(jnp.exp(math.log(2.0) - 1.3862944 * jax.random.uniform(key_list[8], (TOKENS,), jnp.float32) ** steps_of(key_list[8], (TOKENS,), ((0, 16),), -0.2, 0.2)), 0.5, 2.0)
    sample_rows = draw_sample_rows(jax.random.fold_in(key_list[10], 71), 0)
    return dict(hidden_states=hidden_states, head_weight=head_weight, agent_bias=agent_bias, agent_ids=agent_ids, actions=actions, rewards=rewards, values=values, episode_start=episode_start, prior_ratio=prior_ratio, sample_rows=sample_rows)


GAMMA = 0.99
TRACE_DECAY = 0.95
DAMPING = 0.001
RADIUS_SHARE = 0.001

def advantages(rewards, values, episode_start):
    reward_rows = rewards.reshape(-1, SEQ_LEN)
    value_rows = values.reshape(-1, SEQ_LEN)
    start_rows = episode_start.reshape(-1, SEQ_LEN)
    episode_end = jnp.concatenate([start_rows[:, 1:], jnp.ones_like(start_rows[:, :1])], axis=1)
    continues = (1 - episode_end).astype(jnp.float32)
    value_next = jnp.concatenate([value_rows[:, 1:], jnp.zeros_like(value_rows[:, :1])], axis=1)
    temporal = reward_rows + GAMMA * continues * value_next - value_rows

    def backward(running, inputs):
        error, keeps = inputs
        updated = error + GAMMA * TRACE_DECAY * keeps * running
        return (updated, updated)
    final_state, advantage = lax.scan(backward, jnp.zeros((reward_rows.shape[0],), jnp.float32), (temporal.T, continues.T), reverse=True)
    return advantage.T.reshape(-1)

def transpose_product(left, right):
    return lax.dot_general(left, right, (((0,), (0,)), ((), ())), preferred_element_type=jnp.float32)

def reference(hidden_states, head_weight, agent_bias, agent_ids, actions, rewards, values, episode_start, prior_ratio, sample_rows):
    advantage = advantages(rewards, values, episode_start)
    adv_mean = jnp.sum(advantage) / TOKENS
    weight = prior_ratio * (advantage - adv_mean) / TOKENS
    logits = jnp.dot(hidden_states, head_weight, preferred_element_type=jnp.float32) + agent_bias[agent_ids]
    row_peak = lax.optimization_barrier(jnp.max(logits, axis=1, keepdims=True))
    exponent = jnp.exp(logits - row_peak)
    probs = exponent / lax.optimization_barrier(jnp.sum(exponent, axis=1, keepdims=True))
    picked = (actions[:, None] == jnp.arange(A, dtype=jnp.int32)[None, :]).astype(jnp.float32)
    logit_grad = (weight[:, None] * (picked - probs)).astype(jnp.bfloat16)
    grad = transpose_product(hidden_states, logit_grad)
    sampled = hidden_states[sample_rows]
    sprobs = probs[sample_rows]

    def fisher_product(vector):
        lifted = jnp.dot(sampled, vector.astype(jnp.bfloat16), preferred_element_type=jnp.float32)
        centre = lax.optimization_barrier(jnp.sum(sprobs * lifted, axis=1, keepdims=True))
        weighted = (sprobs * (lifted - centre)).astype(jnp.bfloat16)
        return transpose_product(sampled, weighted) / SAMPLES + DAMPING * vector
    solution = jnp.zeros_like(grad)
    resid = grad
    direction = grad
    resid_sq = jnp.sum(resid * resid)
    quad = jnp.float32(0.0)
    for iteration in range(ITERS):
        fisher_image = fisher_product(direction)
        curvature = jnp.sum(direction * fisher_image)
        step_size = resid_sq / curvature
        solution = solution + step_size * direction
        resid = resid - step_size * fisher_image
        quad = quad + step_size * step_size * curvature
        resid_next = jnp.sum(resid * resid)
        direction = resid + resid_next / resid_sq * direction
        resid_sq = resid_next
    return solution * jnp.sqrt(D * A * RADIUS_SHARE / quad)
```

```python
import functools

import jax
import jax.numpy as jnp
from jax import lax
from jax.experimental import pallas as pl
from jax.experimental.pallas import tpu as pltpu
from jax.sharding import PartitionSpec as P

SEQ_LEN = 64
GAMMA = 0.99
TRACE_DECAY = 0.95
DAMPING = 0.001
RADIUS_SHARE = 0.001

F32 = jnp.float32
BF16 = jnp.bfloat16
VMEM_LIMIT = 48 * 1024 * 1024
NT = (((1,), (1,)), ((), ()))
TN = (((0,), (0,)), ((), ()))


def call(kernel, name, **kw):
    return pl.pallas_call(
        kernel, name=name, compiler_params=pltpu.CompilerParams(vmem_limit_bytes=VMEM_LIMIT), **kw
    )


def shape(*dims, dtype=F32):
    return jax.ShapeDtypeStruct(dims, dtype)


def total(x):
    return jnp.sum(jnp.sum(x, axis=1, keepdims=True), axis=0, keepdims=True)


def exchanged(x, code, rows, blocks):
    index = lax.broadcasted_iota(jnp.int32, x.shape, 0)
    bit = 1
    while bit < blocks:
        by = rows * bit
        below = lax.bitwise_and(index, by) == 0
        swapped = jnp.where(below, pltpu.roll(x, x.shape[0] - by, 0), pltpu.roll(x, by, 0))
        x = jnp.where(lax.bitwise_and(code, bit) != 0, swapped, x)
        bit *= 2
    return x


def token_kernel(base_ref, rewards_ref, values_ref, starts_ref, samples_ref, adv_ref, sum_ref, count_ref):
    tokens = rewards_ref.shape[1]
    samples = samples_ref.shape[1]

    def shifted(x, by):
        return pltpu.roll(x, tokens - by, 1)

    lane = lax.broadcasted_iota(jnp.int32, (1, tokens), 1)
    last = lax.rem(lane, SEQ_LEN) == SEQ_LEN - 1
    ends = jnp.where(last, 1.0, shifted(starts_ref[...].astype(F32), 1))
    continues = 1.0 - ends
    values = values_ref[...]
    running = rewards_ref[...] + GAMMA * continues * jnp.where(last, 0.0, shifted(values, 1)) - values
    keeps = GAMMA * TRACE_DECAY * continues
    step = 1
    while step < SEQ_LEN:
        running = running + keeps * shifted(running, step)
        keeps = keeps * shifted(keeps, step)
        step *= 2
    adv_ref[...] = running
    sum_ref[...] = jnp.broadcast_to(jnp.sum(running, axis=1, keepdims=True), sum_ref.shape)

    rows = samples_ref[...] - base_ref[0]
    high = (lax.shift_right_arithmetic(rows, 7) == lax.broadcasted_iota(jnp.int32, (8, samples), 0))
    low = (lax.bitwise_and(rows, 127) == lax.broadcasted_iota(jnp.int32, (128, samples), 0))
    table = lax.dot_general(
        high.astype(F32).astype(BF16), low.astype(F32).astype(BF16), NT, preferred_element_type=F32
    )
    for i in range(tokens // 128):
        count_ref[:, i * 128 : (i + 1) * 128] = table[i : i + 1, :]


def token_work(base, rewards, values, starts, samples):
    tokens = rewards.shape[1]
    assert tokens <= 1024 and tokens % 128 == 0
    vmem = pl.BlockSpec(memory_space=pltpu.VMEM)
    return call(
        token_kernel,
        "token_work",
        in_specs=[pl.BlockSpec(memory_space=pltpu.SMEM)] + [vmem] * 4,
        out_shape=(shape(1, tokens), shape(8, 128), shape(1, tokens)),
    )(base, rewards, values, starts, samples)


def logits_kernel(h_ref, w_ref, bias_ref, ids_ref, exp_ref, stats_ref, acc_ref):
    step = pl.program_id(0)
    product = jnp.dot(h_ref[...], w_ref[...], preferred_element_type=F32)

    @pl.when(step == 0)
    def _():
        acc_ref[...] = product

    @pl.when(step > 0)
    def _():
        acc_ref[...] += product

    @pl.when(step == pl.num_programs(0) - 1)
    def _():
        agents = bias_ref.shape[0]
        tokens = ids_ref.shape[1]
        table = (ids_ref[...] == lax.broadcasted_iota(jnp.int32, (agents, tokens), 0)).astype(F32)
        bias = lax.dot_general(
            bias_ref[...], table, TN, precision=lax.Precision.HIGHEST, preferred_element_type=F32
        )
        logits = acc_ref[...].T + bias
        peak = jnp.max(logits, axis=0, keepdims=True)
        exponent = jnp.exp(logits - peak)
        exp_ref[...] = exponent
        stats_ref[0:1, :] = peak
        stats_ref[1:2, :] = jnp.sum(exponent, axis=0, keepdims=True)
        stats_ref[2:8, :] = jnp.zeros((6, tokens), F32)


def logits_work(hidden, weight, bias, ids, tile):
    tokens, width = hidden.shape
    actions = weight.shape[1]
    return call(
        logits_kernel,
        "logits",
        grid=(width // tile,),
        in_specs=[
            pl.BlockSpec((tokens, tile), lambda j: (0, j)),
            pl.BlockSpec((tile, actions), lambda j: (j, 0)),
            pl.BlockSpec(bias.shape, lambda j: (0, 0)),
            pl.BlockSpec(ids.shape, lambda j: (0, 0)),
        ],
        out_specs=(
            pl.BlockSpec((actions, tokens), lambda j: (0, 0)),
            pl.BlockSpec((8, tokens), lambda j: (0, 0)),
        ),
        out_shape=(shape(actions, tokens), shape(8, tokens)),
        scratch_shapes=[pltpu.VMEM((tokens, actions), F32)],
    )(hidden, weight, bias, ids)


def probs_kernel(blocks, row_count, place_ref, exp_ref, stats_ref, *refs):
    *others, adv_ref, sum_ref, prior_ref, actions_ref, own_p, send_p, own_g, send_g = refs
    half = own_p.shape[0]
    rows = half // blocks
    core, code, first = place_ref[0], place_ref[1], place_ref[2]
    own_peak = stats_ref[0:1, :]
    peak = own_peak
    for other in others:
        peak = jnp.maximum(peak, other[0:1, :])
    denominator = stats_ref[1:2, :] * jnp.exp(own_peak - peak)
    for other in others:
        denominator = denominator + other[1:2, :] * jnp.exp(other[0:1, :] - peak)
    scale = jnp.exp(own_peak - peak) / denominator
    weight = prior_ref[...] * (adv_ref[...] - sum_ref[0:1, 0:1] / row_count) / row_count
    action = actions_ref[...] - first

    def hand_out(part, probs, index, p_ref, g_ref):
        picked = (index == action).astype(F32)
        p_ref[part, :] = probs
        g_ref[part, :] = (weight * (picked - probs)).astype(BF16)

    for side, p_ref, g_ref in ((core, own_p, own_g), (1 - core, send_p, send_g)):
        if rows % 16:
            start = pl.multiple_of(side * half, half)
            probs = exp_ref[pl.ds(start, half), :] * scale
            index = start + lax.broadcasted_iota(jnp.int32, probs.shape, 0)
            probs, index = (exchanged(x, code, rows, blocks) for x in (probs, index))
            hand_out(slice(0, half), probs, index, p_ref, g_ref)
            continue
        for k in range(blocks):
            start = pl.multiple_of(side * half + lax.bitwise_xor(code, k) * rows, rows)
            probs = exp_ref[pl.ds(start, rows), :] * scale
            index = start + lax.broadcasted_iota(jnp.int32, probs.shape, 0)
            hand_out(slice(k * rows, (k + 1) * rows), probs, index, p_ref, g_ref)


def probs_work(blocks, row_count, place, exponent, stats, others, adv, adv_sum, prior, actions):
    count, tokens = exponent.shape
    half = count // 2
    vmem = pl.BlockSpec(memory_space=pltpu.VMEM)
    return call(
        functools.partial(probs_kernel, blocks, row_count),
        "probs",
        in_specs=[pl.BlockSpec(memory_space=pltpu.SMEM)] + [vmem] * (6 + len(others)),
        out_shape=(
            shape(half, tokens),
            shape(half, tokens),
            shape(half, tokens, dtype=BF16),
            shape(half, tokens, dtype=BF16),
        ),
    )(place, exponent, stats, *others, adv, adv_sum, prior, actions)


def outer_kernel(pieces, scale, left0, left1, h0, h1, own_ref, *send_refs):
    product = jnp.dot(left0[...], h0[...], preferred_element_type=F32)
    product = product + jnp.dot(left1[...], h1[...], preferred_element_type=F32)
    if scale != 1.0:
        product = product * scale
    rows = product.shape[0] // sum(len(p) for p in pieces)
    for ref, blocks in zip((own_ref, *send_refs), pieces):
        for i, k in enumerate(blocks):
            ref[i * rows : (i + 1) * rows, :] = product[k * rows : (k + 1) * rows].astype(ref.dtype)


def outer_work(pieces, left, hidden, first, columns, tile, scale, wire):
    rows, tokens = left[0].shape
    blocks = sum(len(p) for p in pieces)
    sizes = [len(p) * (rows // blocks) for p in pieces]
    offset = first // tile
    fixed = pl.BlockSpec((rows, tokens), lambda j: (0, 0))
    moving = pl.BlockSpec((tokens, tile), lambda j: (0, j + offset))
    return call(
        functools.partial(outer_kernel, pieces, scale),
        "outer",
        grid=(columns // tile,),
        in_specs=[fixed, fixed, moving, moving],
        out_specs=[pl.BlockSpec((size, tile), lambda j: (0, j)) for size in sizes],
        out_shape=[
            shape(size, columns, dtype=F32 if i == 0 else wire) for i, size in enumerate(sizes)
        ],
    )(*left, *hidden)


def lift_kernel(with_dots, *refs):
    if with_dots:
        v_ref, h0, h1, p0, p1, g_ref, out_ref, centre_ref, dots_ref, acc = refs
    else:
        v_ref, h0, h1, p0, p1, out_ref, centre_ref, acc = refs
    tokens = h0.shape[0]
    step = pl.program_id(0)
    v = v_ref[...]

    @pl.when(step == 0)
    def _():
        acc[...] = jnp.zeros_like(acc)
        if with_dots:
            dots_ref[...] = jnp.zeros_like(dots_ref)

    acc[:, :tokens] += lax.dot_general(v, h0[...], NT, preferred_element_type=F32)
    acc[:, tokens:] += lax.dot_general(v, h1[...], NT, preferred_element_type=F32)
    if with_dots:
        f = v.astype(F32)
        g = g_ref[...].astype(F32)
        row = lax.broadcasted_iota(jnp.int32, dots_ref.shape, 0)
        dots_ref[...] += jnp.where(
            row == 0, total(g * g), jnp.where(row == 1, total(g * f), jnp.where(row == 2, total(f * f), 0.0))
        )

    @pl.when(step == pl.num_programs(0) - 1)
    def _():
        lifted = acc[...]
        out_ref[...] = lifted
        centre_ref[:, :tokens] = jnp.sum(p0[...] * lifted[:, :tokens], axis=0, keepdims=True)
        centre_ref[:, tokens:] = jnp.sum(p1[...] * lifted[:, tokens:], axis=0, keepdims=True)


def lift_work(v, hidden, probs, tile, grad=None):
    rows, width = v.shape
    tokens = hidden[0].shape[0]
    moving = pl.BlockSpec((rows, tile), lambda j: (0, j))
    states = pl.BlockSpec((tokens, tile), lambda j: (0, j))
    fixed = pl.BlockSpec((rows, tokens), lambda j: (0, 0))
    dots = grad is not None
    return call(
        functools.partial(lift_kernel, dots),
        "lift",
        grid=(width // tile,),
        in_specs=[moving, states, states, fixed, fixed] + [moving] * dots,
        out_specs=[
            pl.BlockSpec((rows, 2 * tokens), lambda j: (0, 0)),
            pl.BlockSpec((1, 2 * tokens), lambda j: (0, 0)),
        ]
        + [pl.BlockSpec((8, 128), lambda j: (0, 0))] * dots,
        out_shape=[shape(rows, 2 * tokens), shape(1, 2 * tokens)] + [shape(8, 128)] * dots,
        scratch_shapes=[pltpu.VMEM((rows, 2 * tokens), F32)],
    )(v, *hidden, *probs, *([grad] if dots else []))


def weighted_kernel(lifted, centre, p0, p1, n0, n1, w0, w1, quad_ref):
    tokens = p0.shape[1]
    quad = jnp.zeros((1, 1), F32)
    for i, (p, n, w) in enumerate(((p0, n0, w0), (p1, n1, w1))):
        part = slice(i * tokens, (i + 1) * tokens)
        spread = lifted[:, part] - centre[:, part]
        weighted = n[...] * p[...] * spread
        w[...] = weighted.astype(BF16)
        quad = quad + total(weighted * spread)
    quad_ref[...] = jnp.broadcast_to(quad, quad_ref.shape)


def weighted_work(lifted, centre, probs, counts):
    rows, tokens = probs[0].shape
    return call(
        weighted_kernel,
        "weighted",
        out_shape=(shape(rows, tokens, dtype=BF16), shape(rows, tokens, dtype=BF16), shape(8, 128)),
    )(lifted, centre, *probs, *counts)


def products_kernel(samples, l1, c1, l2, c2, p0, p1, n0, n1, dots_ref, quad_ref, out_ref):
    tokens = p0.shape[1]
    cross = jnp.zeros((1, 1), F32)
    second = jnp.zeros((1, 1), F32)
    for i, (p, n) in enumerate(((p0, n0), (p1, n1))):
        part = slice(i * tokens, (i + 1) * tokens)
        spread = l2[:, part] - c2[:, part]
        weighted = n[...] * p[...] * spread
        cross = cross + total(weighted * (l1[:, part] - c1[:, part]))
        second = second + total(weighted * spread)
    lane = lax.broadcasted_iota(jnp.int32, out_ref.shape, 1)
    terms = (
        dots_ref[0:1, 0:1],
        dots_ref[1:2, 0:1],
        dots_ref[2:3, 0:1],
        quad_ref[0:1, 0:1] / samples,
        cross / samples,
        second / samples,
    )
    out = jnp.zeros(out_ref.shape, F32)
    for i, term in enumerate(terms):
        out = jnp.where(lane == i, term, out)
    out_ref[...] = out


def products_work(samples, copies, l1, c1, l2, c2, probs, counts, dots, quad):
    return call(
        functools.partial(products_kernel, samples),
        "products",
        out_shape=shape(copies, 128),
    )(l1, c1, l2, c2, *probs, *counts, dots, quad)


def final_kernel(blocks, replicas, size, place_ref, sums_ref, g0, g1, f0, f1, out_ref, acc):
    half = g0.shape[0]
    rows = half // blocks
    core, code = place_ref[0], place_ref[1]
    sums = jnp.sum(sums_ref[...], axis=0, keepdims=True)
    gg, gf, ff = (sums[:, i : i + 1] / replicas for i in range(3))
    q11, q12, q22 = (sums[:, i : i + 1] for i in range(3, 6))
    curvature1 = q11 + DAMPING * gg
    step1 = gg / curvature1
    keep = q11 / curvature1
    rr = keep * keep * gg - 2.0 * keep * step1 * gf + step1 * step1 * ff
    beta = rr / gg
    a = keep + beta
    b = -step1
    curvature2 = a * a * q11 + 2.0 * a * b * q12 + b * b * q22
    curvature2 = curvature2 + DAMPING * (a * a * gg + 2.0 * a * b * gf + b * b * ff)
    step2 = rr / curvature2
    quad = step1 * step1 * curvature1 + step2 * step2 * curvature2
    norm = jnp.sqrt(size * RADIUS_SHARE / quad)
    on_g = norm * (step1 + step2 * a)
    on_f = norm * step2 * b
    for side, g, f in ((core, g0, f0), (1 - core, g1, f1)):
        if rows % 16:
            start = pl.multiple_of(side * half, half)
            both = on_g * g[...].astype(F32) + on_f * f[...].astype(F32)
            acc[pl.ds(start, half), :] = exchanged(both, code, rows, blocks)
            continue
        for k in range(blocks):
            start = pl.multiple_of(side * half + lax.bitwise_xor(code, k) * rows, rows)
            part = slice(k * rows, (k + 1) * rows)
            acc[pl.ds(start, rows), :] = on_g * g[part, :].astype(F32) + on_f * f[part, :].astype(F32)
    out_ref[...] = acc[...].T


def final_work(blocks, replicas, size, place, sums, g, f, tile):
    half, width = g[0].shape
    moving = pl.BlockSpec((half, tile), lambda j: (0, j))
    return call(
        functools.partial(final_kernel, blocks, replicas, size),
        "final",
        grid=(width // tile,),
        in_specs=[
            pl.BlockSpec(memory_space=pltpu.SMEM),
            pl.BlockSpec(sums.shape, lambda j: (0, 0)),
        ]
        + [moving] * 4,
        out_specs=pl.BlockSpec((tile, 2 * half), lambda j: (j, 0)),
        out_shape=shape(width, 2 * half),
        scratch_shapes=[pltpu.VMEM((2 * half, tile), F32)],
    )(place, sums, *g, *f)


def per_device(
    hidden_states,
    head_weight,
    agent_bias,
    agent_ids,
    actions,
    rewards,
    values,
    episode_start,
    prior_ratio,
    sample_rows,
):
    data, model = lax.axis_size("dp"), lax.axis_size("mp")
    index, column = lax.axis_index("dp"), lax.axis_index("mp")
    tokens, width = hidden_states.shape
    local_actions = head_weight.shape[1]
    half = local_actions // 2
    row_count = tokens * data
    samples_all = sample_rows.shape[0] * data
    chips = data // 2
    depth = min(4, chips)
    breadth = chips // depth
    core = lax.rem(index, 2)
    chip = index // 2
    code = lax.rem(chip, breadth) * depth + chip // breadth
    block = half // chips
    tile = 512
    columns_a = 3 * tile
    columns_b = width - columns_a

    def swap(x, slow=0, fast=0, other=0):
        mask = ((slow * breadth + fast) << 1) | other
        return lax.ppermute(x, "dp", [(i, i ^ mask) for i in range(data)])

    def swap_model(x, mask):
        return lax.ppermute(x, "mp", [(i, i ^ mask) for i in range(model)])

    def sum_model(x):
        mask = 1
        while mask < model:
            x = x + swap_model(x, mask)
            mask *= 2
        return x

    def sum_group(x):
        y = swap(x, other=1)
        return sum_model(x + jnp.concatenate([y[:, tokens:], y[:, :tokens]], axis=1))

    def reduce_scatter(left, hidden, scale, wire):
        by_slow = [[f * depth + s for f in range(breadth)] for s in range(depth)]
        by_fast = [[f * depth + s for s in range(depth)] for f in range(breadth)]
        own_b, *send_b = outer_work(by_slow, left, hidden, columns_a, columns_b, tile, scale, wire)
        got_b = [swap(x, slow=i + 1) for i, x in enumerate(send_b)]
        own_a, *send_a = outer_work(by_fast, left, hidden, 0, columns_a, tile, scale, wire)
        got_a = [swap(x, fast=i + 1) for i, x in enumerate(send_a)]
        sum_a = sum((x.astype(F32) for x in got_a), own_a)
        got_a = [
            swap(sum_a[s * block : (s + 1) * block].astype(wire), slow=s) for s in range(1, depth)
        ]
        sum_b = sum((x.astype(F32) for x in got_b), own_b)
        got_b = [
            swap(sum_b[f * block : (f + 1) * block].astype(wire), fast=f) for f in range(1, breadth)
        ]
        sum_a = sum((x.astype(F32) for x in got_a), sum_a[:block])
        sum_b = sum((x.astype(F32) for x in got_b), sum_b[:block])
        return sum_a, sum_b

    def all_gather(part_a, part_b):
        a = jnp.concatenate([part_a] + [swap(part_a, slow=s) for s in range(1, depth)])
        b = jnp.concatenate([part_b] + [swap(part_b, fast=f) for f in range(1, breadth)])
        a = jnp.concatenate([a] + [swap(a, fast=f) for f in range(1, breadth)])
        b = jnp.stack([b] + [swap(b, slow=s) for s in range(1, depth)])
        b = b.reshape(depth, breadth, block, columns_b).transpose(1, 0, 2, 3).reshape(half, columns_b)
        return jnp.concatenate([a, b], axis=1)

    row = lambda x: x.reshape(1, -1)
    place = jnp.stack([core, code, column * local_actions]).astype(jnp.int32)
    base = (index * tokens).astype(jnp.int32).reshape(1)

    adv, adv_sum, counts = token_work(
        base, row(rewards), row(values), row(episode_start), row(sample_rows)
    )
    hidden = (hidden_states, swap(hidden_states, other=1))
    mask = 1
    while mask < data:
        adv_sum = adv_sum + lax.ppermute(adv_sum, "dp", [(i, i ^ mask) for i in range(data)])
        mask *= 2
    exponent, stats = logits_work(hidden_states, head_weight, agent_bias, row(agent_ids), tile)
    others = [swap_model(stats, i) for i in range(1, model)]
    own_p, send_p, own_g, send_g = probs_work(
        chips, row_count, place, exponent, stats, others, adv, adv_sum, row(prior_ratio), row(actions)
    )
    left = (own_g, swap(send_g, other=1))
    probs = (own_p, swap(send_p, other=1))
    counts = (counts, swap(counts, other=1))

    grad_a, grad_b = reduce_scatter(left, hidden, 1.0, BF16)
    grad = all_gather(grad_a.astype(BF16), grad_b.astype(BF16))
    lifted, centre = lift_work(grad, hidden, probs, tile)
    centre = sum_group(centre)
    weighted0, weighted1, quad = weighted_work(lifted, centre, probs, counts)
    image_a, image_b = reduce_scatter((weighted0, weighted1), hidden, 1.0 / samples_all, BF16)
    grad_other = swap(grad, other=1)
    image = all_gather(image_a.astype(BF16), image_b.astype(BF16))
    image_other = swap(image, other=1)
    lifted2, centre2, dots = lift_work(image, hidden, probs, tile, grad)
    centre2 = sum_group(centre2)
    sums = products_work(
        samples_all, data * model, lifted, centre, lifted2, centre2, probs, counts, dots, quad
    )
    sums = lax.all_to_all(sums, ("dp", "mp"), 0, 0, tiled=True)
    size = width * local_actions * model
    return final_work(
        chips, chips, size, place, sums, (grad, grad_other), (image, image_other), tile
    )


def solution(mesh):
    placed = (
        P("dp", None),
        P(None, "mp"),
        P(None, "mp"),
        P("dp"),
        P("dp"),
        P("dp"),
        P("dp"),
        P("dp"),
        P("dp"),
        P("dp"),
    )
    return jax.shard_map(
        per_device, mesh=mesh, in_specs=placed, out_specs=P(None, "mp"), check_vma=False
    )
```
